32 devices in a mesh: row: 4 (over y, x), col: 8 (over z, core).
Axes of the slice: x: 2, y: 2, z: 4, core: 2. Of those that a mesh axis runs over, the one named last changes fastest.
Arguments:
- tokens: bfloat16 [2, 64, 16384], P(None, 'col', 'row'), may hold values from -6 to 6
- gate_weight: bfloat16 [16384, 26624], P(('row', 'col')), may hold values from -0.046875 to 0.046875
- up_weight: bfloat16 [16384, 26624], P(('row', 'col')), may hold values from -0.046875 to 0.046875
- down_weight: bfloat16 [16384, 26624], P(('row', 'col')), may hold values from -0.0390625 to 0.0390625
Outputs:
- block_out: bfloat16 [2, 64, 16384], P(None, 'col', 'row')
The draws below stay inside these ranges and needn't reach their ends.
All inputs are finite; a program needn't handle non-finite values.
Results may differ from the reference program's by a relative error of at most 0.028.
Values may be sent and summed in bfloat16 or wider, within the bound.
No kernel may reach another device: no remote copies, remote signals or barrier semaphores. Data moves between devices by JAX's collectives and lax.ppermute only.
A program may use at most 320 MiB of HBM per device.

```python
import jax
import jax.numpy as jnp
from jax import lax

D = 16384
FF = 26624
MB = 2
TOKENS = 64
N_ROW = 4
N_COL = 8


def block_scale(rng, dims, split, least, top_value):
    gain = 1.0
    for position, blocks in split:
        steps = jax.random.uniform(jax.random.fold_in(jax.random.fold_in(rng, 6), position), (blocks,), jnp.float32, least / len(split), top_value / len(split))
        gain = gain * jnp.repeat(jnp.exp(steps), dims[position] // blocks).reshape((-1,) + (1,) * (len(dims) - 1 - position))
    return gain


def scatter_about(own_key, dims, deviation, most, split=(), dtype=jnp.bfloat16):
    result = jax.random.normal(own_key, dims, jnp.float32) * deviation
    if len(split) > 0:
        result = block_scale(own_key, dims, split, -0.22, 0.18) * result
    return jnp.clip(result, min=-most, max=most).astype(dtype)


def setup_inputs(seed: int = 0) -> dict:
    arg_keys = jax.random.split(jax.random.key(seed), 5)
    tokens = scatter_about(arg_keys[0], (MB, TOKENS, D), 1.0, 6.0, ((1, 8), (2, 4)))
    gate_weight = scatter_about(arg_keys[1], (D, FF), D ** -0.5, 0.046875, ((0, 32),))
    up_weight = scatter_about(arg_keys[2], (D, FF), D ** -0.5, 0.046875, ((0, 32),))
    down_weight = scatter_about(arg_keys[3], (D, FF), FF ** -0.5, 0.0390625, ((0, 32),))
    return {"tokens": tokens, "gate_weight": gate_weight, "up_weight": up_weight, "down_weight": down_weight}


def rounded(value):
    return lax.optimization_barrier(value.astype(jnp.bfloat16)).astype(jnp.float32)


def reference(tokens, gate_weight, up_weight, down_weight):
    row_width = D // N_ROW
    col_width = FF // N_COL
    results = []
    for batch_index in range(MB):
        batch = tokens[batch_index]
        gate = jnp.zeros((TOKENS, FF), jnp.float32)
        up_sum = jnp.zeros((TOKENS, FF), jnp.float32)
        for block in range(N_ROW):
            lower = block * row_width
            piece = batch[:, lower:lower + row_width]
            gate = gate + rounded(jnp.dot(piece, gate_weight[lower:lower + row_width], preferred_element_type=jnp.float32))
            up_sum = up_sum + rounded(jnp.dot(piece, up_weight[lower:lower + row_width], preferred_element_type=jnp.float32))
        hidden = (jax.nn.silu(gate) * up_sum).astype(jnp.bfloat16)
        summed = jnp.zeros((TOKENS, D), jnp.float32)
        for block in range(N_COL):
            lower = block * col_width
            term = lax.dot_general(hidden[:, lower:lower + col_width], down_weight[:, lower:lower + col_width], (((1,), (1,)), ((), ())), preferred_element_type=jnp.float32)
            summed = summed + rounded(term)
        results.append(summed.astype(jnp.bfloat16))
    return jnp.stack(results, 0)
```

```python
import functools

import jax
import jax.numpy as jnp
import numpy as np
from jax import lax
from jax.sharding import PartitionSpec as P

SHARES = (2, 2, 2, 2)
ORDER = (2, 0, 2, 3, 0, 1, 2, 0, 2, 1, 0, 2, 3, 0, 1, 2, 0, 3, 2, 1, 0, 3, 2, 1, 0, 3, 1, 2, 3, 1, 0, 3, 1, 2, 3, 1, 0, 3, 2, 1, 0, 3, 1, 3)

def swap(value, axis, size, bit):
    return lax.ppermute(value, axis, [(i, i ^ bit) for i in range(size)])


def gate_up(x, gate_weight, up_weight, start, width):
    half = x.shape[0] // 2
    parts = [
        jnp.dot(
            x, lax.slice_in_dim(weight, start, start + width, axis=1),
            preferred_element_type=jnp.float32,
        ).astype(jnp.bfloat16)
        for weight in (gate_weight, up_weight)
    ]
    return [p[:half] for p in parts], [p[half:] for p in parts]


def down(own, other, down_weight, before, start):
    hidden = jnp.concatenate([own, other], 0)
    weight = lax.slice_in_dim(down_weight, start, start + own.shape[1], axis=1)
    return before + lax.dot_general(
        hidden, weight, (((1,), (1,)), ((), ())), preferred_element_type=jnp.float32
    )


def add_halves(keep, received, axis):
    half = keep.shape[axis] // 2
    sides = []
    for k in range(2):
        kept = lax.slice_in_dim(keep, k * half, (k + 1) * half, axis=axis).astype(jnp.float32)
        came = lax.slice_in_dim(received, k * half, (k + 1) * half, axis=axis).astype(jnp.float32)
        sides.append((kept + came).astype(jnp.bfloat16))
    return sides


def step_order(pairs, steps):
    if len(ORDER) == pairs * steps:
        return ORDER
    return [p for t in range(steps + 2 * pairs) for p in range(pairs) if 0 <= t - 2 * p < steps]


def on_device(n_row, n_col, tokens, gate_weight, up_weight, down_weight):
    batches, local_tokens, local_features = tokens.shape
    own_tokens = batches * local_tokens
    all_tokens = own_tokens * n_col
    features, units = gate_weight.shape
    per_device = own_tokens // n_row
    row, col = lax.axis_index("row"), lax.axis_index("col")
    row_bits = [1 << k for k in range(n_row.bit_length() - 1)]
    col_bits = [1 << k for k in range(1, n_col.bit_length() - 1)]
    core_bit = 1
    orders = (row_bits, row_bits[::-1])

    x = tokens.reshape(own_tokens, local_features)
    for bit in col_bits[::-1] + [core_bit]:
        half = x.shape[1] // 2
        low, high = x[:, :half], x[:, half:]
        mine = (col & bit) != 0
        keep, send = jnp.where(mine, high, low), jnp.where(mine, low, high)
        x = jnp.concatenate([keep, swap(send, "col", n_col, bit)], 0)

    base = np.arange(all_tokens).reshape(
        (2,) + (2,) * len(col_bits) + (2,) * len(row_bits) + (per_device,)
    )
    n_cb, n_rb = len(col_bits), len(row_bits)
    sources = []
    for order in orders:
        row_dims = [1 + n_cb + n_rb - 1 - row_bits.index(bit) for bit in order]
        dims = [0] + row_dims + list(range(1, 1 + n_cb)) + [1 + n_cb + n_rb]
        sources.append(base.transpose(dims).reshape(-1))
    source = jnp.asarray(np.concatenate(sources), jnp.int32) ^ (row * per_device)
    pick = source[:, None] == lax.broadcasted_iota(jnp.int32, (2 * all_tokens, all_tokens), 1)
    ordered = jnp.dot(pick.astype(jnp.bfloat16), x, preferred_element_type=jnp.float32).astype(
        jnp.bfloat16
    )
    x_orders = (ordered[:all_tokens], ordered[all_tokens:])

    totals = [jnp.zeros((all_tokens, features), jnp.float32) for _ in orders]
    last = [x]

    def after(*values):
        return lax.optimization_barrier((values, last[0]))[0]

    def steps(starts, width):
        sums = []
        for k in range(2):
            (x_now,) = after(x_orders[k])
            keep, send = gate_up(x_now, gate_weight, up_weight, starts[k], width)
            last[0] = send
            came = [swap(part, "col", n_col, core_bit) for part in send]
            sums.append((keep, came))
        yield
        for stage in range(n_rb):
            for k in range(2):
                if stage == 0:
                    (kept_gate, kept_up), (came_gate, came_up) = after(*sums[k])
                    halves = add_halves(kept_gate, came_gate, 0), add_halves(kept_up, came_up, 0)
                    keep, send = (jnp.stack(side) for side in zip(*halves))
                else:
                    keep, send = add_halves(*after(*sums[k]), 1)
                last[0] = send
                sums[k] = keep, swap(send, "row", n_row, orders[k][stage])
            yield
        keep, received = (jnp.stack(parts) for parts in zip(*(after(*s) for s in sums)))
        for bit in col_bits:
            keep, send = add_halves(keep, received, 2)
            last[0] = send
            received = swap(send, "col", n_col, bit)
            yield
            keep, received = after(keep, received)
        total = keep.astype(jnp.float32) + received.astype(jnp.float32)
        hidden = (jax.nn.silu(total[:, 0]) * total[:, 1]).astype(jnp.bfloat16)
        for bit in col_bits[::-1]:
            last[0] = hidden
            received = swap(hidden, "col", n_col, bit)
            yield
            hidden = jnp.concatenate(after(hidden, received), 1)
        parts = [hidden[k] for k in range(2)]
        for stage in range(n_rb):
            came = []
            for k in range(2):
                last[0] = parts[k]
                came.append(swap(parts[k], "row", n_row, orders[k][n_rb - 1 - stage]))
            yield
            for k in range(2):
                parts[k] = jnp.concatenate(after(parts[k], came[k]), 0)
        others = []
        for k in range(2):
            last[0] = parts[k]
            others.append(swap(parts[k], "col", n_col, core_bit))
        yield
        for k in range(2):
            own, other = after(parts[k], others[k])
            totals[k] = last[0] = down(own, other, down_weight, totals[k], starts[k])

    share = units // (2 * sum(SHARES))
    ends = np.cumsum(SHARES) * share
    half_units = units // 2
    running = [
        steps([int(end) - n * share, half_units + int(end) - n * share], n * share)
        for n, end in zip(SHARES, ends)
    ]
    for pair in step_order(len(SHARES), 3 + 2 * n_rb + 2 * n_cb):
        next(running[pair], None)

    total = jnp.concatenate(totals, 0)
    out = lax.dot_general(
        pick.astype(jnp.float32), total, (((0,), (0,)), ((), ())),
        precision=lax.Precision.HIGHEST, preferred_element_type=jnp.float32,
    ).astype(jnp.bfloat16)

    for bit in [core_bit] + col_bits:
        half = out.shape[0] // 2
        keep, came = out[:half], swap(out[half:], "col", n_col, bit)
        mine = (col & bit) != 0
        out = jnp.concatenate([jnp.where(mine, came, keep), jnp.where(mine, keep, came)], 1)
    return out.reshape(batches, local_tokens, local_features)


def solution(mesh):
    in_specs = (
        P(None, "col", "row"),
        P(("row", "col"), None),
        P(("row", "col"), None),
        P(("row", "col"), None),
    )
    out_specs = P(None, "col", "row")
    body = functools.partial(on_device, mesh.shape["row"], mesh.shape["col"])
    return jax.shard_map(body, mesh=mesh, in_specs=in_specs, out_specs=out_specs, check_vma=False)
```

```python
import functools

import jax
import jax.numpy as jnp
import numpy as np
from jax import lax
from jax.sharding import PartitionSpec as P

SHARES = (4, 4, 4, 4)
ORDER = (1, 3, 1, 0, 3, 1, 2, 3, 0, 1, 2, 3, 1, 3, 1, 0, 3, 1, 2, 3, 0, 1, 2, 3, 0, 1, 2, 0, 3, 2, 0, 1, 2, 0, 3, 2, 0, 2, 1, 0, 3, 2, 0, 2)


def step_order(chunks, steps):
    if len(ORDER) == chunks * steps:
        return ORDER
    return [c for t in range(steps + 2 * chunks) for c in range(chunks) if 0 <= t - 2 * c < steps]


def gate_up(x, gate_weight, up_weight, start, width):
    half = x.shape[0] // 2
    parts = [
        jnp.dot(
            x, lax.slice_in_dim(weight, start, start + width, axis=1),
            preferred_element_type=jnp.float32,
        ).astype(jnp.bfloat16)
        for weight in (gate_weight, up_weight)
    ]
    return [p[:half] for p in parts], [p[half:] for p in parts]


def down(own, other, down_weight, before, start):
    hidden = jnp.concatenate([own, other], 0)
    weight = lax.slice_in_dim(down_weight, start, start + own.shape[1], axis=1)
    return before + lax.dot_general(
        hidden, weight, (((1,), (1,)), ((), ())), preferred_element_type=jnp.float32
    )


def add_halves(keep, received, axis):
    half = keep.shape[axis] // 2
    sides = []
    for k in range(2):
        kept = lax.slice_in_dim(keep, k * half, (k + 1) * half, axis=axis).astype(jnp.float32)
        came = lax.slice_in_dim(received, k * half, (k + 1) * half, axis=axis).astype(jnp.float32)
        sides.append((kept + came).astype(jnp.bfloat16))
    return sides


def on_device(n_row, n_col, tokens, gate_weight, up_weight, down_weight):
    batches, local_tokens, local_features = tokens.shape
    own_tokens = batches * local_tokens
    all_tokens = own_tokens * n_col
    features, units = gate_weight.shape
    per_device = own_tokens // n_row
    row, col = lax.axis_index("row"), lax.axis_index("col")
    core = 1
    col_bits = [1 << k for k in range(1, n_col.bit_length() - 1)]
    row_bits = [n_col << k for k in range(n_row.bit_length() - 1)]
    orders = (row_bits + col_bits, row_bits[::-1] + col_bits[::-1])
    stages = list(zip(*orders))

    def swap(value, bits):
        pairs = [(d, d ^ bits[d & core]) for d in range(n_row * n_col)]
        return lax.ppermute(value, ("row", "col"), pairs)

    x = tokens.reshape(own_tokens, local_features)
    for bit in col_bits[::-1] + [core]:
        half = x.shape[1] // 2
        low, high = x[:, :half], x[:, half:]
        mine = (col & bit) != 0
        keep, send = jnp.where(mine, high, low), jnp.where(mine, low, high)
        x = jnp.concatenate([keep, swap(send, (bit, bit))], 0)

    weight = {bit: all_tokens >> (k + 1) for k, bit in enumerate([core] + col_bits)}
    weight.update({bit: bit // n_col * per_device for bit in row_bits})

    def half_source(order):
        rows = np.zeros(1, np.int32)
        for bit in order:
            rows = (rows[:, None] + np.array([0, weight[bit]])).reshape(-1)
        return (rows[:, None] + np.arange(per_device)).reshape(-1)

    own_first = [
        np.concatenate([half_source(orders[k]), weight[core] + half_source(orders[1 - k])])
        for k in range(2)
    ]
    source = jnp.where((col & core) == 0, *(jnp.asarray(s, jnp.int32) for s in own_first))
    source = source ^ (row * per_device)
    pick = source[:, None] == lax.broadcasted_iota(jnp.int32, (all_tokens, all_tokens), 1)
    x = jnp.dot(pick.astype(jnp.bfloat16), x, preferred_element_type=jnp.float32).astype(jnp.bfloat16)

    total = [jnp.zeros((all_tokens, features), jnp.float32)]
    last = [x]

    def after(*values):
        return lax.optimization_barrier((values, last[0]))[0]

    def steps(start, width):
        (x_now,) = after(x)
        keep, send = gate_up(x_now, gate_weight, up_weight, start, width)
        last[0] = send
        received = [swap(part, (core, core)) for part in send]
        yield
        keep, received = after(keep, received)
        halves = [add_halves(k, r, 0) for k, r in zip(keep, received)]
        keep, send = (jnp.stack(side) for side in zip(*halves))
        for n, bits in enumerate(stages):
            if n > 0:
                keep, send = add_halves(*after(keep, received), 1)
            last[0] = send
            received = swap(send, bits)
            yield
        keep, received = after(keep, received)
        both = keep.astype(jnp.float32) + received.astype(jnp.float32)
        hidden = (jax.nn.silu(both[0]) * both[1]).astype(jnp.bfloat16)
        for bits in stages[::-1]:
            last[0] = hidden
            received = swap(hidden, bits)
            yield
            hidden = jnp.concatenate(after(hidden, received), 0)
        last[0] = hidden
        other = swap(hidden, (core, core))
        yield
        own, other = after(hidden, other)
        total[0] = last[0] = down(own, other, down_weight, total[0], start)

    share = units // sum(SHARES)
    ends = np.cumsum(SHARES) * share
    running = [steps(int(end) - n * share, n * share) for n, end in zip(SHARES, ends)]
    for chunk in step_order(len(SHARES), 3 + 2 * len(stages)):
        next(running[chunk], None)

    out = lax.dot_general(
        pick.astype(jnp.float32), total[0], (((0,), (0,)), ((), ())),
        precision=lax.Precision.HIGHEST, preferred_element_type=jnp.float32,
    ).astype(jnp.bfloat16)

    for bit in [core] + col_bits:
        half = out.shape[0] // 2
        keep, came = out[:half], swap(out[half:], (bit, bit))
        mine = (col & bit) != 0
        out = jnp.concatenate([jnp.where(mine, came, keep), jnp.where(mine, keep, came)], 1)
    return out.reshape(batches, local_tokens, local_features)


def solution(mesh):
    in_specs = (
        P(None, "col", "row"),
        P(("row", "col"), None),
        P(("row", "col"), None),
        P(("row", "col"), None),
    )
    out_specs = P(None, "col", "row")
    body = functools.partial(on_device, mesh.shape["row"], mesh.shape["col"])
    return jax.shard_map(body, mesh=mesh, in_specs=in_specs, out_specs=out_specs, check_vma=False)
```

```python
import functools

import jax
import jax.numpy as jnp
import numpy as np
from jax import lax
from jax.experimental import pallas as pl
from jax.experimental.pallas import tpu as pltpu
from jax.sharding import PartitionSpec as P

VMEM_BYTES = 40 * 2**20
SHARES = (3, 4, 4, 3, 2)
ORDER = (1, 3, 1, 3, 2, 1, 4, 2, 3, 1, 0, 2, 1, 4, 3, 0, 2, 1, 3, 4, 2, 0, 1, 4, 3, 0, 2, 1, 4, 3, 0, 2, 4, 1, 3, 0, 4, 2, 3, 0, 1, 4, 2, 0, 3, 4, 2, 0, 4, 0)


def step_order(chunks, steps):
    if len(ORDER) == chunks * steps:
        return ORDER
    return [c for t in range(steps + 2 * chunks) for c in range(chunks) if 0 <= t - 2 * c < steps]


def cut(weight, start, width):
    return lax.slice_in_dim(weight, start, start + width, axis=1)


def block_width(width, most):
    for blocks in range(1, width // 128 + 1):
        if width % (128 * blocks) == 0 and width // blocks <= most:
            return width // blocks
    return width


def gate_up_kernel(start, x_ref, gate_ref, up_ref, keep_ref, send_ref, held, arrived):
    step = pl.program_id(0)
    block = keep_ref.shape[2]
    half = keep_ref.shape[1]

    def copy(n, k):
        columns = pl.ds(pl.multiple_of(start + n * block, 128), block)
        return pltpu.make_async_copy((gate_ref, up_ref)[k].at[:, columns], held.at[n, k], arrived.at[n, k])

    @pl.when(step == 0)
    def _():
        for n in range(held.shape[0]):
            for k in range(2):
                copy(n, k).start()

    for k in range(2):
        copy(step, k).wait()
        part = jnp.dot(x_ref[...], held[step, k], preferred_element_type=jnp.float32).astype(jnp.bfloat16)
        keep_ref[k] = part[:half]
        send_ref[k] = part[half:]


def gate_up(x, gate_weight, up_weight, start, width):
    tokens, depth = x.shape
    block = block_width(width, 1664)
    blocks = width // block
    out_spec = pl.BlockSpec((2, tokens // 2, block), lambda n: (0, 0, n))
    out_shape = jax.ShapeDtypeStruct((2, tokens // 2, width), jnp.bfloat16)
    return pl.pallas_call(
        functools.partial(gate_up_kernel, start),
        grid=(blocks,),
        in_specs=[
            pl.BlockSpec((tokens, depth), lambda n: (0, 0)),
            pl.BlockSpec(memory_space=pl.ANY),
            pl.BlockSpec(memory_space=pl.ANY),
        ],
        out_specs=[out_spec, out_spec],
        out_shape=[out_shape, out_shape],
        scratch_shapes=[
            pltpu.VMEM((blocks, 2, depth, block), jnp.bfloat16),
            pltpu.SemaphoreType.DMA((blocks, 2)),
        ],
        compiler_params=pltpu.CompilerParams(vmem_limit_bytes=VMEM_BYTES),
        cost_estimate=pl.CostEstimate(flops=0, bytes_accessed=0, transcendentals=0),
    )(x, gate_weight, up_weight)


def down(own, other, down_weight, before, start):
    hidden = jnp.concatenate([own, other], 0)
    weight = cut(down_weight, start, own.shape[1])
    return before + lax.dot_general(
        hidden, weight, (((1,), (1,)), ((), ())), preferred_element_type=jnp.float32
    )


def add_halves(keep, received, axis):
    half = keep.shape[axis] // 2
    sides = []
    for k in range(2):
        kept = lax.slice_in_dim(keep, k * half, (k + 1) * half, axis=axis).astype(jnp.float32)
        came = lax.slice_in_dim(received, k * half, (k + 1) * half, axis=axis).astype(jnp.float32)
        sides.append((kept + came).astype(jnp.bfloat16))
    return sides


def on_device(n_row, n_col, tokens, gate_weight, up_weight, down_weight):
    batches, local_tokens, local_features = tokens.shape
    own_tokens = batches * local_tokens
    all_tokens = own_tokens * n_col
    features, units = gate_weight.shape
    per_device = own_tokens // n_row
    row, col = lax.axis_index("row"), lax.axis_index("col")
    device = row * n_col + col
    core = 1
    col_bits = [1 << k for k in range(1, n_col.bit_length() - 1)]
    row_bits = [n_col << k for k in range(n_row.bit_length() - 1)]
    orders = (row_bits + col_bits, row_bits[::-1] + col_bits[::-1])
    stages = list(zip(*orders))

    def swap(value, bits):
        pairs = [(d, d ^ bits[d & core]) for d in range(n_row * n_col)]
        return lax.ppermute(value, ("row", "col"), pairs)

    on_upper = (col & core) != 0
    others = n_col // 2

    def turn(blocks):
        for k in range(others.bit_length() - 1):
            turned = jnp.stack([blocks[i ^ (1 << k)] for i in range(others)])
            blocks = jnp.where((col & (2 << k)) != 0, turned, blocks)
        return blocks

    def exchange(blocks):
        return [blocks[0]] + [swap(blocks[s], (2 * s, 2 * s)) for s in range(1, others)]

    x = tokens.reshape(own_tokens, local_features)
    lower, upper = (
        jnp.stack([cut(x, (2 * i + k) * features, features) for i in range(others)]) for k in range(2)
    )
    keep, send = jnp.where(on_upper, upper, lower), jnp.where(on_upper, lower, upper)
    x = jnp.concatenate([keep, swap(send, (core, core))], 1)
    x = jnp.concatenate(exchange(turn(x)), 0)

    weight = {core: own_tokens}
    weight.update({bit: bit * own_tokens for bit in col_bits})
    weight.update({bit: bit // n_col * per_device for bit in row_bits})

    def half_source(order):
        rows = np.zeros(1, np.int32)
        for bit in order:
            rows = (rows[:, None] + np.array([0, weight[bit]])).reshape(-1)
        return (rows[:, None] + np.arange(per_device)).reshape(-1)

    own_first = [
        np.concatenate([half_source(orders[k]), weight[core] + half_source(orders[1 - k])])
        for k in range(2)
    ]
    source = jnp.where(on_upper, *(jnp.asarray(own_first[k], jnp.int32) for k in (1, 0)))
    lasts = [jnp.where((device & o[-1]) != 0, weight[o[-1]], 0) for o in orders]
    own_last, other_last = jnp.where(on_upper, lasts[1], lasts[0]), jnp.where(on_upper, *lasts)
    is_own = np.arange(all_tokens) < all_tokens // 2
    source = source ^ (row * per_device) ^ jnp.where(is_own, own_last, other_last)
    pick = source[:, None] == lax.broadcasted_iota(jnp.int32, (all_tokens, all_tokens), 1)
    x = jnp.dot(pick.astype(jnp.bfloat16), x, preferred_element_type=jnp.float32).astype(jnp.bfloat16)

    total = [jnp.zeros((all_tokens, features), jnp.float32)]
    last = [x]

    def after(*values):
        return lax.optimization_barrier((values, last[0]))[0]

    def steps(start, width):
        (x_now,) = after(x)
        keep, send = gate_up(x_now, gate_weight, up_weight, start, width)
        last[0] = send
        received = swap(send, (core, core))
        yield
        for n, bits in enumerate(stages[:-1]):
            keep, send = add_halves(*after(keep, received), 1)
            last[0] = send
            received = swap(send, bits)
            yield
        keep, received = after(keep, received)
        whole = (keep.astype(jnp.float32) + received.astype(jnp.float32)).astype(jnp.bfloat16)
        last[0] = whole
        received = swap(whole, stages[-1])
        yield
        whole, received = after(whole, received)
        both = whole.astype(jnp.float32) + received.astype(jnp.float32)
        hidden = (jax.nn.silu(both[0]) * both[1]).astype(jnp.bfloat16)
        for bits in stages[-2::-1]:
            last[0] = hidden
            received = swap(hidden, bits)
            yield
            hidden = jnp.concatenate(after(hidden, received), 0)
        last[0] = hidden
        other = swap(hidden, (core, core))
        yield
        own, other = after(hidden, other)
        total[0] = last[0] = down(own, other, down_weight, total[0], start)

    share = units // sum(SHARES)
    ends = np.cumsum(SHARES) * share
    running = [steps(int(end) - n * share, n * share) for n, end in zip(SHARES, ends)]
    for chunk in step_order(len(SHARES), 2 + 2 * len(stages)):
        next(running[chunk], None)

    out = lax.dot_general(
        pick.astype(jnp.float32), total[0], (((0,), (0,)), ((), ())),
        precision=lax.Precision.HIGHEST, preferred_element_type=jnp.float32,
    ).astype(jnp.bfloat16)

    out = jnp.stack(exchange(out.reshape(others, 2 * own_tokens, features)))
    keep, came = out[:, :own_tokens], swap(out[:, own_tokens:], (core, core))
    lower, upper = turn(jnp.where(on_upper, came, keep)), turn(jnp.where(on_upper, keep, came))
    out = jnp.concatenate([side[i] for i in range(others) for side in (lower, upper)], 1)
    return out.reshape(batches, local_tokens, local_features)


def solution(mesh):
    in_specs = (
        P(None, "col", "row"),
        P(("row", "col"), None),
        P(("row", "col"), None),
        P(("row", "col"), None),
    )
    out_specs = P(None, "col", "row")
    body = functools.partial(on_device, mesh.shape["row"], mesh.shape["col"])
    return jax.shard_map(body, mesh=mesh, in_specs=in_specs, out_specs=out_specs, check_vma=False)
```

```python
import functools

import jax
import jax.numpy as jnp
import numpy as np
from jax import lax
from jax.experimental import pallas as pl
from jax.experimental.pallas import tpu as pltpu
from jax.sharding import PartitionSpec as P

VMEM_BYTES = 28 * 2**20
SHARES = (3,4,4,3,2)
ORDER = (2, 4, 2, 1, 4, 2, 1, 0, 4, 2, 3, 1, 2, 0, 4, 3, 1, 2, 4, 0, 1, 2, 4, 3, 0, 1, 4, 3, 2, 0, 1, 3, 4, 0, 2, 1, 3, 0, 2, 3, 0, 4, 1, 3, 1, 0, 4, 3, 0, 3)


def step_order(chunks, steps):
    if len(ORDER) == chunks * steps:
        return ORDER
    return [c for t in range(steps + 2 * chunks) for c in range(chunks) if 0 <= t - 2 * c < steps]


def cut(weight, start, width):
    return lax.slice_in_dim(weight, start, start + width, axis=1)


def block_width(width, most):
    for blocks in range(1, width // 128 + 1):
        if width % (128 * blocks) == 0 and width // blocks <= most:
            return width // blocks
    return width


def gate_up_kernel(start, x_ref, gate_ref, up_ref, keep_ref, send_ref, held, arrived):
    step = pl.program_id(0)
    block = keep_ref.shape[2]
    half = keep_ref.shape[1]

    def copy(n, k):
        columns = pl.ds(pl.multiple_of(start + n * block, 128), block)
        return pltpu.make_async_copy((gate_ref, up_ref)[k].at[:, columns], held.at[n, k], arrived.at[n, k])

    @pl.when(step == 0)
    def _():
        for n in range(held.shape[0]):
            for k in range(2):
                copy(n, k).start()

    for k in range(2):
        copy(step, k).wait()
        part = jnp.dot(x_ref[...], held[step, k], preferred_element_type=jnp.float32).astype(jnp.bfloat16)
        keep_ref[k] = part[:half]
        send_ref[k] = part[half:]


def gate_up(x, gate_weight, up_weight, start, width):
    tokens, depth = x.shape
    block = block_width(width, 1664)
    blocks = width // block
    out_spec = pl.BlockSpec((2, tokens // 2, block), lambda n: (0, 0, n))
    out_shape = jax.ShapeDtypeStruct((2, tokens // 2, width), jnp.bfloat16)
    return pl.pallas_call(
        functools.partial(gate_up_kernel, start),
        grid=(blocks,),
        in_specs=[
            pl.BlockSpec((tokens, depth), lambda n: (0, 0)),
            pl.BlockSpec(memory_space=pl.ANY),
            pl.BlockSpec(memory_space=pl.ANY),
        ],
        out_specs=[out_spec, out_spec],
        out_shape=[out_shape, out_shape],
        scratch_shapes=[
            pltpu.VMEM((blocks, 2, depth, block), jnp.bfloat16),
            pltpu.SemaphoreType.DMA((blocks, 2)),
        ],
        compiler_params=pltpu.CompilerParams(vmem_limit_bytes=VMEM_BYTES),
        cost_estimate=pl.CostEstimate(flops=0, bytes_accessed=0, transcendentals=0),
    )(x, gate_weight, up_weight)


def fetch_kernel(start, gate_ref, up_ref, held_ref, arrived):
    columns = pl.ds(start, held_ref.shape[2])
    copies = [
        pltpu.make_async_copy(ref.at[:, columns], held_ref.at[k], arrived.at[k])
        for k, ref in enumerate((gate_ref, up_ref))
    ]
    for copy in copies:
        copy.start()
    for copy in copies:
        copy.wait()


def fetch(gate_weight, up_weight, start, width):
    held = (2, gate_weight.shape[0], width)
    return pl.pallas_call(
        functools.partial(fetch_kernel, start),
        in_specs=[pl.BlockSpec(memory_space=pl.ANY)] * 2,
        out_specs=pl.BlockSpec(memory_space=pltpu.VMEM),
        out_shape=pltpu.VMEM(held, jnp.bfloat16),
        scratch_shapes=[pltpu.SemaphoreType.DMA((2,))],
        compiler_params=pltpu.CompilerParams(vmem_limit_bytes=VMEM_BYTES),
        cost_estimate=pl.CostEstimate(flops=0, bytes_accessed=0, transcendentals=0),
    )(gate_weight, up_weight)


def gate_up_held_kernel(x_ref, held_ref, keep_ref, send_ref):
    half, width = keep_ref.shape[1:]
    block = block_width(width, 1664)
    for n in range(0, width, block):
        for k in range(2):
            part = jnp.dot(
                x_ref[...], held_ref[k, :, n : n + block], preferred_element_type=jnp.float32
            ).astype(jnp.bfloat16)
            keep_ref[k, :, n : n + block] = part[:half]
            send_ref[k, :, n : n + block] = part[half:]


def gate_up_held(x, held):
    tokens, width = x.shape[0], held.shape[2]
    out_shape = jax.ShapeDtypeStruct((2, tokens // 2, width), jnp.bfloat16)
    in_vmem = pl.BlockSpec(memory_space=pltpu.VMEM)
    return pl.pallas_call(
        gate_up_held_kernel,
        in_specs=[in_vmem, in_vmem],
        out_specs=[in_vmem, in_vmem],
        out_shape=[out_shape, out_shape],
        compiler_params=pltpu.CompilerParams(vmem_limit_bytes=VMEM_BYTES),
        cost_estimate=pl.CostEstimate(flops=0, bytes_accessed=0, transcendentals=0),
    )(x, held)


def down(own, other, down_weight, before, start):
    hidden = jnp.concatenate([own, other], 0)
    weight = cut(down_weight, start, own.shape[1])
    return before + lax.dot_general(
        hidden, weight, (((1,), (1,)), ((), ())), preferred_element_type=jnp.float32
    )


def add_halves(keep, received, axis):
    half = keep.shape[axis] // 2
    sides = []
    for k in range(2):
        kept = lax.slice_in_dim(keep, k * half, (k + 1) * half, axis=axis).astype(jnp.float32)
        came = lax.slice_in_dim(received, k * half, (k + 1) * half, axis=axis).astype(jnp.float32)
        sides.append((kept + came).astype(jnp.bfloat16))
    return sides


def on_device(n_row, n_col, tokens, gate_weight, up_weight, down_weight):
    batches, local_tokens, local_features = tokens.shape
    own_tokens = batches * local_tokens
    all_tokens = own_tokens * n_col
    features, units = gate_weight.shape
    per_device = own_tokens // n_row
    row, col = lax.axis_index("row"), lax.axis_index("col")
    device = row * n_col + col
    core = 1
    col_bits = [1 << k for k in range(1, n_col.bit_length() - 1)]
    row_bits = [n_col << k for k in range(n_row.bit_length() - 1)]
    orders = (row_bits + col_bits, row_bits[::-1] + col_bits[::-1])
    stages = list(zip(*orders))

    def swap(value, bits):
        pairs = [(d, d ^ bits[d & core]) for d in range(n_row * n_col)]
        return lax.ppermute(value, ("row", "col"), pairs)

    on_upper = (col & core) != 0
    others = n_col // 2

    def turn(blocks):
        for k in range(others.bit_length() - 1):
            turned = jnp.stack([blocks[i ^ (1 << k)] for i in range(others)])
            blocks = jnp.where((col & (2 << k)) != 0, turned, blocks)
        return blocks

    def exchange(blocks):
        return [blocks[0]] + [swap(blocks[s], (2 * s, 2 * s)) for s in range(1, others)]

    x = tokens.reshape(own_tokens, local_features)
    lower, upper = (
        jnp.stack([cut(x, (2 * i + k) * features, features) for i in range(others)]) for k in range(2)
    )
    keep, send = jnp.where(on_upper, upper, lower), jnp.where(on_upper, lower, upper)
    x = jnp.concatenate([keep, swap(send, (core, core))], 1)
    x = jnp.concatenate(exchange(turn(x)), 0)

    weight = {core: own_tokens}
    weight.update({bit: bit * own_tokens for bit in col_bits})
    weight.update({bit: bit // n_col * per_device for bit in row_bits})

    def half_source(order):
        rows = np.zeros(1, np.int32)
        for bit in order:
            rows = (rows[:, None] + np.array([0, weight[bit]])).reshape(-1)
        return (rows[:, None] + np.arange(per_device)).reshape(-1)

    own_first = [
        np.concatenate([half_source(orders[k]), weight[core] + half_source(orders[1 - k])])
        for k in range(2)
    ]
    source = jnp.where(on_upper, *(jnp.asarray(own_first[k], jnp.int32) for k in (1, 0)))
    lasts = [jnp.where((device & o[-1]) != 0, weight[o[-1]], 0) for o in orders]
    own_last, other_last = jnp.where(on_upper, lasts[1], lasts[0]), jnp.where(on_upper, *lasts)
    is_own = np.arange(all_tokens) < all_tokens // 2
    source = source ^ (row * per_device) ^ jnp.where(is_own, own_last, other_last)
    pick = source[:, None] == lax.broadcasted_iota(jnp.int32, (all_tokens, all_tokens), 1)
    x = jnp.dot(pick.astype(jnp.bfloat16), x, preferred_element_type=jnp.float32).astype(jnp.bfloat16)

    total = [jnp.zeros((all_tokens, features), jnp.float32)]
    last = [x]

    def after(*values):
        return lax.optimization_barrier((values, last[0]))[0]

    def steps(start, width, held):
        (x_now,) = after(x)
        if held is None:
            keep, send = gate_up(x_now, gate_weight, up_weight, start, width)
        else:
            keep, send = gate_up_held(x_now, held)
        last[0] = send
        received = swap(send, (core, core))
        yield
        for n, bits in enumerate(stages[:-1]):
            keep, send = add_halves(*after(keep, received), 1)
            last[0] = send
            received = swap(send, bits)
            yield
        keep, received = after(keep, received)
        whole = (keep.astype(jnp.float32) + received.astype(jnp.float32)).astype(jnp.bfloat16)
        last[0] = whole
        received = swap(whole, stages[-1])
        yield
        whole, received = after(whole, received)
        both = whole.astype(jnp.float32) + received.astype(jnp.float32)
        hidden = (jax.nn.silu(both[0]) * both[1]).astype(jnp.bfloat16)
        for bits in stages[-2::-1]:
            last[0] = hidden
            received = swap(hidden, bits)
            yield
            hidden = jnp.concatenate(after(hidden, received), 0)
        last[0] = hidden
        other = swap(hidden, (core, core))
        yield
        own, other = after(hidden, other)
        total[0] = last[0] = down(own, other, down_weight, total[0], start)

    share = units // sum(SHARES)
    ends = np.cumsum(SHARES) * share
    turns = step_order(len(SHARES), 2 + 2 * len(stages))
    running = []
    for chunk, (n, end) in enumerate(zip(SHARES, ends)):
        start, width = int(end) - n * share, n * share
        held = fetch(gate_weight, up_weight, start, width) if chunk == turns[0] else None
        running.append(steps(start, width, held))
    for chunk in turns:
        next(running[chunk], None)

    out = lax.dot_general(
        pick.astype(jnp.float32), total[0], (((0,), (0,)), ((), ())),
        precision=lax.Precision.HIGHEST, preferred_element_type=jnp.float32,
    ).astype(jnp.bfloat16)

    out = jnp.stack(exchange(out.reshape(others, 2 * own_tokens, features)))
    keep, came = out[:, :own_tokens], swap(out[:, own_tokens:], (core, core))
    lower, upper = turn(jnp.where(on_upper, came, keep)), turn(jnp.where(on_upper, keep, came))
    out = jnp.concatenate([side[i] for i in range(others) for side in (lower, upper)], 1)
    return out.reshape(batches, local_tokens, local_features)


def solution(mesh):
    in_specs = (
        P(None, "col", "row"),
        P(("row", "col"), None),
        P(("row", "col"), None),
        P(("row", "col"), None),
    )
    out_specs = P(None, "col", "row")
    body = functools.partial(on_device, mesh.shape["row"], mesh.shape["col"])
    return jax.shard_map(body, mesh=mesh, in_specs=in_specs, out_specs=out_specs, check_vma=False)
```

```python
import functools

import jax
import jax.numpy as jnp
import numpy as np
from jax import lax
from jax.experimental import pallas as pl
from jax.experimental.pallas import tpu as pltpu
from jax.sharding import PartitionSpec as P

VMEM_BYTES = 28 * 2**20
SHARES = (4, 4, 3, 2, 3)
PLANS = (0, 0, 0, 0, 1)
ORDER = (0, 3, 0, 4, 3, 2, 4, 0, 2, 1, 3, 0, 1, 4, 2, 0, 3, 1, 4, 2, 0, 3, 1, 4, 2, 0, 3, 4, 1, 0, 2, 4, 3, 1, 2, 3, 0, 4, 1, 2, 0, 1, 3, 4, 2, 3, 4, 1, 2, 1)


def step_order(chunks, steps):
    if len(ORDER) == chunks * steps:
        return ORDER
    return [c for t in range(steps + 2 * chunks) for c in range(chunks) if 0 <= t - 2 * c < steps]


def cut(weight, start, width):
    return lax.slice_in_dim(weight, start, start + width, axis=1)


def block_width(width, most):
    for blocks in range(1, width // 128 + 1):
        if width % (128 * blocks) == 0 and width // blocks <= most:
            return width // blocks
    return width


def gate_up_kernel(start, x_ref, gate_ref, up_ref, keep_ref, send_ref, held, arrived):
    step = pl.program_id(0)
    block = keep_ref.shape[2]
    half = keep_ref.shape[1]

    def copy(n, k):
        columns = pl.ds(pl.multiple_of(start + n * block, 128), block)
        return pltpu.make_async_copy((gate_ref, up_ref)[k].at[:, columns], held.at[n, k], arrived.at[n, k])

    @pl.when(step == 0)
    def _():
        for n in range(held.shape[0]):
            for k in range(2):
                copy(n, k).start()

    for k in range(2):
        copy(step, k).wait()
        part = jnp.dot(x_ref[...], held[step, k], preferred_element_type=jnp.float32).astype(jnp.bfloat16)
        keep_ref[k] = part[:half]
        send_ref[k] = part[half:]


def gate_up(x, gate_weight, up_weight, start, width):
    tokens, depth = x.shape
    block = block_width(width, 1664)
    blocks = width // block
    out_spec = pl.BlockSpec((2, tokens // 2, block), lambda n: (0, 0, n))
    out_shape = jax.ShapeDtypeStruct((2, tokens // 2, width), jnp.bfloat16)
    return pl.pallas_call(
        functools.partial(gate_up_kernel, start),
        grid=(blocks,),
        in_specs=[
            pl.BlockSpec((tokens, depth), lambda n: (0, 0)),
            pl.BlockSpec(memory_space=pl.ANY),
            pl.BlockSpec(memory_space=pl.ANY),
        ],
        out_specs=[out_spec, out_spec],
        out_shape=[out_shape, out_shape],
        scratch_shapes=[
            pltpu.VMEM((blocks, 2, depth, block), jnp.bfloat16),
            pltpu.SemaphoreType.DMA((blocks, 2)),
        ],
        compiler_params=pltpu.CompilerParams(vmem_limit_bytes=VMEM_BYTES),
        cost_estimate=pl.CostEstimate(flops=0, bytes_accessed=0, transcendentals=0),
    )(x, gate_weight, up_weight)


def fetch_kernel(start, gate_ref, up_ref, held_ref, arrived):
    columns = pl.ds(start, held_ref.shape[2])
    copies = [
        pltpu.make_async_copy(ref.at[:, columns], held_ref.at[k], arrived.at[k])
        for k, ref in enumerate((gate_ref, up_ref))
    ]
    for copy in copies:
        copy.start()
    for copy in copies:
        copy.wait()


def fetch(gate_weight, up_weight, start, width):
    held = (2, gate_weight.shape[0], width)
    return pl.pallas_call(
        functools.partial(fetch_kernel, start),
        in_specs=[pl.BlockSpec(memory_space=pl.ANY)] * 2,
        out_specs=pl.BlockSpec(memory_space=pltpu.VMEM),
        out_shape=pltpu.VMEM(held, jnp.bfloat16),
        scratch_shapes=[pltpu.SemaphoreType.DMA((2,))],
        compiler_params=pltpu.CompilerParams(vmem_limit_bytes=VMEM_BYTES),
        cost_estimate=pl.CostEstimate(flops=0, bytes_accessed=0, transcendentals=0),
    )(gate_weight, up_weight)


def gate_up_held_kernel(x_ref, held_ref, keep_ref, send_ref):
    half, width = keep_ref.shape[1:]
    block = block_width(width, 1664)
    for n in range(0, width, block):
        for k in range(2):
            part = jnp.dot(
                x_ref[...], held_ref[k, :, n : n + block], preferred_element_type=jnp.float32
            ).astype(jnp.bfloat16)
            keep_ref[k, :, n : n + block] = part[:half]
            send_ref[k, :, n : n + block] = part[half:]


def gate_up_held(x, held):
    tokens, width = x.shape[0], held.shape[2]
    out_shape = jax.ShapeDtypeStruct((2, tokens // 2, width), jnp.bfloat16)
    in_vmem = pl.BlockSpec(memory_space=pltpu.VMEM)
    return pl.pallas_call(
        gate_up_held_kernel,
        in_specs=[in_vmem, in_vmem],
        out_specs=[in_vmem, in_vmem],
        out_shape=[out_shape, out_shape],
        compiler_params=pltpu.CompilerParams(vmem_limit_bytes=VMEM_BYTES),
        cost_estimate=pl.CostEstimate(flops=0, bytes_accessed=0, transcendentals=0),
    )(x, held)


def down(own, other, down_weight, before, start):
    hidden = jnp.concatenate([own, other], 0)
    weight = cut(down_weight, start, own.shape[1])
    return before + lax.dot_general(
        hidden, weight, (((1,), (1,)), ((), ())), preferred_element_type=jnp.float32
    )


def add_halves(keep, received, axis):
    half = keep.shape[axis] // 2
    sides = []
    for k in range(2):
        kept = lax.slice_in_dim(keep, k * half, (k + 1) * half, axis=axis).astype(jnp.float32)
        came = lax.slice_in_dim(received, k * half, (k + 1) * half, axis=axis).astype(jnp.float32)
        sides.append((kept + came).astype(jnp.bfloat16))
    return sides


def on_device(n_row, n_col, tokens, gate_weight, up_weight, down_weight):
    batches, local_tokens, local_features = tokens.shape
    own_tokens = batches * local_tokens
    all_tokens = own_tokens * n_col
    features, units = gate_weight.shape
    per_device = own_tokens // n_row
    row, col = lax.axis_index("row"), lax.axis_index("col")
    device = row * n_col + col
    core = 1
    col_bits = [1 << k for k in range(1, n_col.bit_length() - 1)]
    row_bits = [n_col << k for k in range(n_row.bit_length() - 1)]
    plans = (
        (row_bits + col_bits, row_bits[::-1] + col_bits[::-1]),
        (col_bits + row_bits, col_bits[::-1] + row_bits[::-1]),
    )

    def swap(value, bits):
        pairs = [(d, d ^ bits[d & core]) for d in range(n_row * n_col)]
        return lax.ppermute(value, ("row", "col"), pairs)

    on_upper = (col & core) != 0
    others = n_col // 2

    def turn(blocks):
        for k in range(others.bit_length() - 1):
            turned = jnp.stack([blocks[i ^ (1 << k)] for i in range(others)])
            blocks = jnp.where((col & (2 << k)) != 0, turned, blocks)
        return blocks

    def exchange(blocks):
        return [blocks[0]] + [swap(blocks[s], (2 * s, 2 * s)) for s in range(1, others)]

    x = tokens.reshape(own_tokens, local_features)
    lower, upper = (
        jnp.stack([cut(x, (2 * i + k) * features, features) for i in range(others)]) for k in range(2)
    )
    keep, send = jnp.where(on_upper, upper, lower), jnp.where(on_upper, lower, upper)
    x = jnp.concatenate([keep, swap(send, (core, core))], 1)
    x = jnp.concatenate(exchange(turn(x)), 0)

    weight = {core: own_tokens}
    weight.update({bit: bit * own_tokens for bit in col_bits})
    weight.update({bit: bit // n_col * per_device for bit in row_bits})

    def half_source(order):
        rows = np.zeros(1, np.int32)
        for bit in order:
            rows = (rows[:, None] + np.array([0, weight[bit]])).reshape(-1)
        return (rows[:, None] + np.arange(per_device)).reshape(-1)

    def scattered(orders):
        own_first = [
            np.concatenate([half_source(orders[k]), weight[core] + half_source(orders[1 - k])])
            for k in range(2)
        ]
        source = jnp.where(on_upper, *(jnp.asarray(own_first[k], jnp.int32) for k in (1, 0)))
        lasts = [jnp.where((device & o[-1]) != 0, weight[o[-1]], 0) for o in orders]
        own_last, other_last = jnp.where(on_upper, lasts[1], lasts[0]), jnp.where(on_upper, *lasts)
        is_own = np.arange(all_tokens) < all_tokens // 2
        return source ^ (row * per_device) ^ jnp.where(is_own, own_last, other_last)

    source = jnp.concatenate([scattered(orders) for orders in plans])
    pick = source[:, None] == lax.broadcasted_iota(jnp.int32, (len(plans) * all_tokens, all_tokens), 1)
    placed = jnp.dot(pick.astype(jnp.bfloat16), x, preferred_element_type=jnp.float32).astype(jnp.bfloat16)

    totals = [jnp.zeros((all_tokens, features), jnp.float32) for _ in plans]
    last = [placed]

    def after(*values):
        return lax.optimization_barrier((values, last[0]))[0]

    def steps(plan, start, width, held):
        stages = list(zip(*plans[plan]))
        (x_now,) = after(placed[plan * all_tokens : (plan + 1) * all_tokens])
        if held is None:
            keep, send = gate_up(x_now, gate_weight, up_weight, start, width)
        else:
            keep, send = gate_up_held(x_now, held)
        last[0] = send
        received = swap(send, (core, core))
        yield
        for n, bits in enumerate(stages[:-1]):
            keep, send = add_halves(*after(keep, received), 1)
            last[0] = send
            received = swap(send, bits)
            yield
        keep, received = after(keep, received)
        whole = (keep.astype(jnp.float32) + received.astype(jnp.float32)).astype(jnp.bfloat16)
        last[0] = whole
        received = swap(whole, stages[-1])
        yield
        whole, received = after(whole, received)
        both = whole.astype(jnp.float32) + received.astype(jnp.float32)
        hidden = (jax.nn.silu(both[0]) * both[1]).astype(jnp.bfloat16)
        for bits in stages[-2::-1]:
            last[0] = hidden
            received = swap(hidden, bits)
            yield
            hidden = jnp.concatenate(after(hidden, received), 0)
        last[0] = hidden
        other = swap(hidden, (core, core))
        yield
        own, other = after(hidden, other)
        totals[plan] = last[0] = down(own, other, down_weight, totals[plan], start)

    share = units // sum(SHARES)
    ends = np.cumsum(SHARES) * share
    turns = step_order(len(SHARES), 2 + 2 * len(plans[0][0]))
    running = []
    for chunk, (n, end) in enumerate(zip(SHARES, ends)):
        start, width = int(end) - n * share, n * share
        held = fetch(gate_weight, up_weight, start, width) if chunk == turns[0] else None
        running.append(steps(PLANS[chunk], start, width, held))
    for chunk in turns:
        next(running[chunk], None)

    out = lax.dot_general(
        pick.astype(jnp.float32), jnp.concatenate(totals, 0), (((0,), (0,)), ((), ())),
        precision=lax.Precision.HIGHEST, preferred_element_type=jnp.float32,
    ).astype(jnp.bfloat16)

    out = jnp.stack(exchange(out.reshape(others, 2 * own_tokens, features)))
    keep, came = out[:, :own_tokens], swap(out[:, own_tokens:], (core, core))
    lower, upper = turn(jnp.where(on_upper, came, keep)), turn(jnp.where(on_upper, keep, came))
    out = jnp.concatenate([side[i] for i in range(others) for side in (lower, upper)], 1)
    return out.reshape(batches, local_tokens, local_features)


def solution(mesh):
    in_specs = (
        P(None, "col", "row"),
        P(("row", "col"), None),
        P(("row", "col"), None),
        P(("row", "col"), None),
    )
    out_specs = P(None, "col", "row")
    body = functools.partial(on_device, mesh.shape["row"], mesh.shape["col"])
    return jax.shard_map(body, mesh=mesh, in_specs=in_specs, out_specs=out_specs, check_vma=False)
```

```python
import functools

import jax
import jax.numpy as jnp
import numpy as np
from jax import lax
from jax.experimental import pallas as pl
from jax.experimental.pallas import tpu as pltpu
from jax.sharding import PartitionSpec as P

VMEM_BYTES = 28 * 2**20
SHARES = (4, 4, 3, 2, 3)
PLANS = (0, 0, 0, 0, 1)
ORDER = (0, 4, 0, 3, 4, 3, 1, 0, 3, 1, 4, 2, 0, 3, 2, 1, 0, 4, 3, 2, 0, 1, 4, 3, 2, 0, 1, 3, 4, 2, 0, 1, 4, 3, 2, 1, 0, 4, 3, 2, 1, 0, 2, 4, 3, 1, 4, 2, 1, 2)


def step_order(chunks, steps):
    if len(ORDER) == chunks * steps:
        return ORDER
    return [c for t in range(steps + 2 * chunks) for c in range(chunks) if 0 <= t - 2 * c < steps]


def cut(weight, start, width):
    return lax.slice_in_dim(weight, start, start + width, axis=1)


def block_width(width, most):
    for blocks in range(1, width // 128 + 1):
        if width % (128 * blocks) == 0 and width // blocks <= most:
            return width // blocks
    return width


def gate_up_kernel(start, x_ref, gate_ref, up_ref, keep_ref, send_ref, held, arrived):
    step = pl.program_id(0)
    block = keep_ref.shape[2]
    half = keep_ref.shape[1]

    def copy(n, k):
        columns = pl.ds(pl.multiple_of(start + n * block, 128), block)
        return pltpu.make_async_copy((gate_ref, up_ref)[k].at[:, columns], held.at[n, k], arrived.at[n, k])

    @pl.when(step == 0)
    def _():
        for n in range(held.shape[0]):
            for k in range(2):
                copy(n, k).start()

    for k in range(2):
        copy(step, k).wait()
        part = jnp.dot(x_ref[...], held[step, k], preferred_element_type=jnp.float32).astype(jnp.bfloat16)
        keep_ref[k] = part[:half]
        send_ref[k] = part[half:]


def gate_up(x, gate_weight, up_weight, start, width):
    tokens, depth = x.shape
    block = block_width(width, 1664)
    blocks = width // block
    out_spec = pl.BlockSpec((2, tokens // 2, block), lambda n: (0, 0, n))
    out_shape = jax.ShapeDtypeStruct((2, tokens // 2, width), jnp.bfloat16)
    return pl.pallas_call(
        functools.partial(gate_up_kernel, start),
        grid=(blocks,),
        in_specs=[
            pl.BlockSpec((tokens, depth), lambda n: (0, 0)),
            pl.BlockSpec(memory_space=pl.ANY),
            pl.BlockSpec(memory_space=pl.ANY),
        ],
        out_specs=[out_spec, out_spec],
        out_shape=[out_shape, out_shape],
        scratch_shapes=[
            pltpu.VMEM((blocks, 2, depth, block), jnp.bfloat16),
            pltpu.SemaphoreType.DMA((blocks, 2)),
        ],
        compiler_params=pltpu.CompilerParams(vmem_limit_bytes=VMEM_BYTES),
        cost_estimate=pl.CostEstimate(flops=0, bytes_accessed=0, transcendentals=0),
    )(x, gate_weight, up_weight)


def fetch_kernel(start, gate_ref, up_ref, held_ref, arrived):
    columns = pl.ds(start, held_ref.shape[2])
    copies = [
        pltpu.make_async_copy(ref.at[:, columns], held_ref.at[k], arrived.at[k])
        for k, ref in enumerate((gate_ref, up_ref))
    ]
    for copy in copies:
        copy.start()
    for copy in copies:
        copy.wait()


def fetch(gate_weight, up_weight, start, width):
    held = (2, gate_weight.shape[0], width)
    return pl.pallas_call(
        functools.partial(fetch_kernel, start),
        in_specs=[pl.BlockSpec(memory_space=pl.ANY)] * 2,
        out_specs=pl.BlockSpec(memory_space=pltpu.VMEM),
        out_shape=pltpu.VMEM(held, jnp.bfloat16),
        scratch_shapes=[pltpu.SemaphoreType.DMA((2,))],
        compiler_params=pltpu.CompilerParams(vmem_limit_bytes=VMEM_BYTES),
        cost_estimate=pl.CostEstimate(flops=0, bytes_accessed=0, transcendentals=0),
    )(gate_weight, up_weight)


def gate_up_held_kernel(x_ref, held_ref, keep_ref, send_ref):
    half, width = keep_ref.shape[1:]
    block = block_width(width, 1664)
    for n in range(0, width, block):
        for k in range(2):
            part = jnp.dot(
                x_ref[...], held_ref[k, :, n : n + block], preferred_element_type=jnp.float32
            ).astype(jnp.bfloat16)
            keep_ref[k, :, n : n + block] = part[:half]
            send_ref[k, :, n : n + block] = part[half:]


def gate_up_held(x, held):
    tokens, width = x.shape[0], held.shape[2]
    out_shape = jax.ShapeDtypeStruct((2, tokens // 2, width), jnp.bfloat16)
    in_vmem = pl.BlockSpec(memory_space=pltpu.VMEM)
    return pl.pallas_call(
        gate_up_held_kernel,
        in_specs=[in_vmem, in_vmem],
        out_specs=[in_vmem, in_vmem],
        out_shape=[out_shape, out_shape],
        compiler_params=pltpu.CompilerParams(vmem_limit_bytes=VMEM_BYTES),
        cost_estimate=pl.CostEstimate(flops=0, bytes_accessed=0, transcendentals=0),
    )(x, held)


def down(own, other, down_weight, before, start):
    hidden = jnp.concatenate([own, other], 0)
    weight = cut(down_weight, start, own.shape[1])
    return before + lax.dot_general(
        hidden, weight, (((1,), (1,)), ((), ())), preferred_element_type=jnp.float32
    )


def add_halves(keep, received, axis):
    half = keep.shape[axis] // 2
    sides = []
    for k in range(2):
        kept = lax.slice_in_dim(keep, k * half, (k + 1) * half, axis=axis).astype(jnp.float32)
        came = lax.slice_in_dim(received, k * half, (k + 1) * half, axis=axis).astype(jnp.float32)
        sides.append((kept + came).astype(jnp.bfloat16))
    return sides


def on_device(n_row, n_col, tokens, gate_weight, up_weight, down_weight):
    batches, local_tokens, local_features = tokens.shape
    own_tokens = batches * local_tokens
    all_tokens = own_tokens * n_col
    features, units = gate_weight.shape
    per_device = own_tokens // n_row
    row, col = lax.axis_index("row"), lax.axis_index("col")
    device = row * n_col + col
    core = 1
    col_bits = [1 << k for k in range(1, n_col.bit_length() - 1)]
    row_bits = [n_col << k for k in range(n_row.bit_length() - 1)]
    plans = (
        (row_bits + col_bits, row_bits[::-1] + col_bits[::-1]),
        (col_bits + row_bits, col_bits[::-1] + row_bits[::-1]),
    )

    def swap(value, bits):
        pairs = [(d, d ^ bits[d & core]) for d in range(n_row * n_col)]
        return lax.ppermute(value, ("row", "col"), pairs)

    on_upper = (col & core) != 0
    others = n_col // 2

    def turn(blocks):
        for k in range(others.bit_length() - 1):
            turned = jnp.stack([blocks[i ^ (1 << k)] for i in range(others)])
            blocks = jnp.where((col & (2 << k)) != 0, turned, blocks)
        return blocks

    def exchange(blocks):
        return [blocks[0]] + [swap(blocks[s], (2 * s, 2 * s)) for s in range(1, others)]

    x = tokens.reshape(own_tokens, local_features)
    lower, upper = (
        jnp.stack([cut(x, (2 * i + k) * features, features) for i in range(others)]) for k in range(2)
    )
    keep, send = jnp.where(on_upper, upper, lower), jnp.where(on_upper, lower, upper)
    x = jnp.concatenate([keep, swap(send, (core, core))], 1)
    x = jnp.concatenate(exchange(turn(x)), 0)

    weight = {core: own_tokens}
    weight.update({bit: bit * own_tokens for bit in col_bits})
    weight.update({bit: bit // n_col * per_device for bit in row_bits})

    def half_source(order):
        rows = np.zeros(1, np.int32)
        for bit in order:
            rows = (rows[:, None] + np.array([0, weight[bit]])).reshape(-1)
        return (rows[:, None] + np.arange(per_device)).reshape(-1)

    def scattered(orders):
        own_first = [
            np.concatenate([half_source(orders[k]), weight[core] + half_source(orders[1 - k])])
            for k in range(2)
        ]
        source = jnp.where(on_upper, *(jnp.asarray(own_first[k], jnp.int32) for k in (1, 0)))
        lasts = [jnp.where((device & o[-1]) != 0, weight[o[-1]], 0) for o in orders]
        own_last, other_last = jnp.where(on_upper, lasts[1], lasts[0]), jnp.where(on_upper, *lasts)
        is_own = np.arange(all_tokens) < all_tokens // 2
        return source ^ (row * per_device) ^ jnp.where(is_own, own_last, other_last)

    source = jnp.concatenate([scattered(orders) for orders in plans])
    pick = source[:, None] == lax.broadcasted_iota(jnp.int32, (len(plans) * all_tokens, all_tokens), 1)
    placed = jnp.dot(pick.astype(jnp.bfloat16), x, preferred_element_type=jnp.float32).astype(jnp.bfloat16)

    totals = [jnp.zeros((all_tokens, features), jnp.float32) for _ in plans]
    last = [placed]

    def after(*values):
        return lax.optimization_barrier((values, last[0]))[0]

    def steps(plan, start, width, held):
        stages = list(zip(*plans[plan]))
        (x_now,) = after(placed[plan * all_tokens : (plan + 1) * all_tokens])
        if held is None:
            keep, send = gate_up(x_now, gate_weight, up_weight, start, width)
        else:
            keep, send = gate_up_held(x_now, held)
        last[0] = send
        received = swap(send, (core, core))
        yield
        for n, bits in enumerate(stages[:-1]):
            keep, send = add_halves(*after(keep, received), 1)
            last[0] = send
            received = swap(send, bits)
            yield
        keep, received = after(keep, received)
        whole = (keep.astype(jnp.float32) + received.astype(jnp.float32)).astype(jnp.bfloat16)
        last[0] = whole
        received = swap(whole, stages[-1])
        yield
        whole, received = after(whole, received)
        both = whole.astype(jnp.float32) + received.astype(jnp.float32)
        hidden = (jax.nn.silu(both[0]) * both[1]).astype(jnp.bfloat16)
        for bits in stages[-2::-1]:
            last[0] = hidden
            received = swap(hidden, bits)
            yield
            hidden = jnp.concatenate(after(hidden, received), 0)
        last[0] = hidden
        other = swap(hidden, (core, core))
        yield
        own, other = after(hidden, other)
        totals[plan] = last[0] = down(own, other, down_weight, totals[plan], start)

    share = units // sum(SHARES)
    ends = np.cumsum(SHARES) * share
    turns = step_order(len(SHARES), 2 + 2 * len(plans[0][0]))
    running = []
    for chunk, (n, end) in enumerate(zip(SHARES, ends)):
        start, width = int(end) - n * share, n * share
        held = fetch(gate_weight, up_weight, start, width) if chunk == turns[0] else None
        running.append(steps(PLANS[chunk], start, width, held))
    for chunk in turns:
        next(running[chunk], None)

    out = lax.dot_general(
        pick.astype(jnp.float32), jnp.concatenate(totals, 0), (((0,), (0,)), ((), ())),
        precision=lax.Precision.HIGHEST, preferred_element_type=jnp.float32,
    ).astype(jnp.bfloat16)

    out = jnp.stack(exchange(out.reshape(others, 2 * own_tokens, features)))
    keep, came = out[:, :own_tokens], swap(out[:, own_tokens:], (core, core))
    lower, upper = turn(jnp.where(on_upper, came, keep)), turn(jnp.where(on_upper, keep, came))
    out = jnp.concatenate([side[i] for i in range(others) for side in (lower, upper)], 1)
    return out.reshape(batches, local_tokens, local_features)


def solution(mesh):
    in_specs = (
        P(None, "col", "row"),
        P(("row", "col"), None),
        P(("row", "col"), None),
        P(("row", "col"), None),
    )
    out_specs = P(None, "col", "row")
    body = functools.partial(on_device, mesh.shape["row"], mesh.shape["col"])
    return jax.shard_map(body, mesh=mesh, in_specs=in_specs, out_specs=out_specs, check_vma=False)
```
